32 devices in a mesh: ctx: 8 (over z, x), head: 2 (over y), dp: 2 (over core).
Axes of the slice: x: 2, y: 2, z: 4, core: 2. Of those that a mesh axis runs over, the one named last changes fastest.
Arguments:
- query: bfloat16 [2, 4096, 5120], P('dp', 'ctx', 'head'), may hold values from -6 to 6
- key: bfloat16 [2, 4096, 1024], P('dp', 'ctx', 'head'), may hold values from -6 to 6
- value: bfloat16 [2, 4096, 1024], P('dp', 'ctx', 'head'), may hold values from -6 to 6
- output: bfloat16 [2, 4096, 5120], P('dp', 'ctx', 'head'), may hold values from -1.796875 to 1.796875
- output_gradient: bfloat16 [2, 4096, 5120], P('dp', 'ctx', 'head'), may hold values from -96 to 96
- parent: int32 [2, 8], P('dp'), may hold values from -1 to 6, as said below
- owner: int32 [2, 8], P('dp'), may hold values from 0 to 7, each once within a row
Outputs:
- d_query: bfloat16 [2, 4096, 5120], P('dp', 'ctx', 'head')
- d_key: bfloat16 [2, 4096, 1024], P('dp', 'ctx', 'head')
- d_value: bfloat16 [2, 4096, 1024], P('dp', 'ctx', 'head')
- bias_q_grad: float32 [5120], P('head')
- bias_k_grad: float32 [1024], P('head')
- bias_v_grad: float32 [1024], P('head')
The draws below stay inside these ranges and needn't reach their ends.
Inputs may be any that keep to these rules, and one draw needn't show every extreme that they name: In each tree, tiles 0 to 0 form the prompt, each with parent t - 1 (tile 0 has -1); the later tiles form 4 consecutive runs (responses) of 1 or 2 tiles, some run of 2 in every tree; a run's first tile has as parent the last prompt tile, its second tile has the run's first tile.
All inputs are finite; a program needn't handle non-finite values.
Results may differ from the reference program's by a relative error of at most 0.005.
Values may be sent and summed in bfloat16 or wider, within the bound.
No kernel may reach another device: no remote copies, remote signals or barrier semaphores. Data moves between devices by JAX's collectives and lax.ppermute only.
A program may use at most 128 MiB of HBM per device.

```python
import jax
import jax.numpy as jnp
from jax import lax

QUERY_HEADS = 40
KEY_HEADS = 8
HEAD_WIDTH = 128
MASK_TILE = 512
QUERY_PER_KV = 5
PROMPT_TREES = 2
TREE_TILES = 8
TREE_TOKENS = 4096
PROMPT_TILES = 1
RESPONSES = 4
RESP_TILES = 7


def drawn_pair(key):
    base = jax.random.fold_in(key, 17)
    key_q, key_k = jax.random.split(base, 2)
    query_layout = (PROMPT_TREES, TREE_TOKENS, KEY_HEADS, QUERY_PER_KV, HEAD_WIDTH)
    key_layout = (PROMPT_TREES, TREE_TOKENS, KEY_HEADS, HEAD_WIDTH)
    query_rows = jnp.clip(jax.random.normal(key_q, query_layout, jnp.float32), -6.0, 6.0)
    key_rows = jnp.clip(jax.random.normal(key_k, key_layout, jnp.float32), -6.0, 6.0)
    return (query_rows.reshape(PROMPT_TREES, TREE_TOKENS, QUERY_HEADS * HEAD_WIDTH), key_rows.reshape(PROMPT_TREES, TREE_TOKENS, KEY_HEADS * HEAD_WIDTH))


def draw_query(key, part):
    return drawn_pair(key)[0].astype(jnp.bfloat16)


def draw_key(key, part):
    return drawn_pair(key)[1].astype(jnp.bfloat16)


def draw_parent(key, part):

    def one_tree(subkey):
        order = jax.random.permutation(subkey, RESPONSES).astype(jnp.int32)
        lengths = 1 + (order < RESP_TILES - RESPONSES).astype(jnp.int32)
        starts = PROMPT_TILES + jnp.cumsum(lengths) - lengths
        tiles = jnp.arange(TREE_TILES, dtype=jnp.int32)
        first = jnp.any(tiles[:, None] == starts[None, :], axis=1)
        first = jnp.logical_and(first, tiles >= PROMPT_TILES)
        return jnp.where(first, PROMPT_TILES - 1, tiles - 1).astype(jnp.int32)
    return jax.vmap(one_tree)(jax.random.split(jax.random.fold_in(key, 3), PROMPT_TREES))


def block_levels(own_key, extent, shards, least, high):
    loudness, own = 1.0, jax.random.fold_in(own_key, 6)
    for position, parts in shards:
        steps = jnp.exp(jax.random.uniform(jax.random.fold_in(own, position), (parts,), jnp.float32, least / len(shards), high / len(shards)))
        loudness = loudness * jnp.repeat(steps, extent[position] // parts).reshape([-1 if axis == position else 1 for axis in range(len(extent))])
    return loudness


def centred(key, dims, width, limit, cuts=(), kind=jnp.bfloat16):
    factor_of = block_levels(key, dims, cuts, -0.22, 0.18) if cuts else 1.0
    entries = jax.random.normal(key, dims, jnp.float32) * width * factor_of
    return jnp.minimum(jnp.maximum(entries, -limit), limit).astype(kind)


def setup_inputs(seed: int = 0) -> dict:
    key_of = jax.random.split(jax.random.key(seed), 8)
    return {
        "query": draw_query(jax.random.fold_in(key_of[7], 71), 0),
        "key": draw_key(jax.random.fold_in(key_of[7], 71), 0),
        "value": centred(key_of[2], (PROMPT_TREES, TREE_TOKENS, KEY_HEADS * HEAD_WIDTH), 1.0, 6.0, ((0, 2), (1, 8), (2, 2))),
        "output": centred(key_of[3], (PROMPT_TREES, TREE_TOKENS, QUERY_HEADS * HEAD_WIDTH), 0.3, 1.796875, ((0, 2), (1, 8), (2, 2))),
        "output_gradient": centred(key_of[4], (PROMPT_TREES, TREE_TOKENS, QUERY_HEADS * HEAD_WIDTH), 16.0, 96.0, ((0, 2), (1, 8), (2, 2))),
        "parent": draw_parent(jax.random.fold_in(key_of[7], 71), 0),
        "owner": jax.vmap(lambda own: jax.random.permutation(own, TREE_TILES))(jax.random.split(key_of[6], PROMPT_TREES)).reshape((PROMPT_TREES, TREE_TILES)).astype(jnp.int32),
    }


NEGATIVE_FILL = -1e30


def tree_tables(parent_row, owner_row):
    count = parent_row.shape[0]
    tiles = jnp.arange(count, dtype=jnp.int32)
    tile_at = jnp.sum(jnp.where(owner_row[None, :] == tiles[:, None], tiles[None, :], 0), axis=1).astype(jnp.int32)

    def climb(step, state):
        reach, current = state
        match = current[:, None] == tiles[None, :]
        reach = jnp.logical_or(reach, match)
        upward = jnp.sum(jnp.where(match, parent_row[None, :], 0), axis=1)
        upward = jnp.where(current < 0, -1, upward).astype(jnp.int32)
        return reach, upward

    reach, _ = lax.fori_loop(0, count, climb, (jnp.zeros((count, count), bool), tiles))
    select = (tile_at[:, None] == tiles[None, :]).astype(jnp.float32)
    packed = jnp.dot(jnp.dot(select, reach.astype(jnp.float32), precision=lax.Precision.HIGHEST), select.T, precision=lax.Precision.HIGHEST)
    seen = (packed > 0.5).astype(jnp.int32)
    return tile_at, seen


def one_tree(query, key, value, output, output_gradient, seen, trained):
    scale_factor = HEAD_WIDTH ** -0.5
    high = lax.Precision.HIGHEST
    query_grouped5 = query.reshape(TREE_TILES, MASK_TILE, KEY_HEADS, QUERY_PER_KV, HEAD_WIDTH).astype(jnp.float32)
    gradient_grouped5 = output_gradient.reshape(TREE_TILES, MASK_TILE, KEY_HEADS, QUERY_PER_KV, HEAD_WIDTH).astype(jnp.float32)
    output_grouped5 = output.reshape(TREE_TILES, MASK_TILE, KEY_HEADS, QUERY_PER_KV, HEAD_WIDTH).astype(jnp.float32)
    key_tensor4 = key.reshape(TREE_TILES, MASK_TILE, KEY_HEADS, HEAD_WIDTH).astype(jnp.float32)
    value_tensor4 = value.reshape(TREE_TILES, MASK_TILE, KEY_HEADS, HEAD_WIDTH).astype(jnp.float32)
    causal = jnp.arange(MASK_TILE)[:, None] >= jnp.arange(MASK_TILE)[None, :]

    def scores_of(i, j):
        scores = jnp.einsum('ignd,jgd->gnij', query_grouped5[i], key_tensor4[j], precision=high) * scale_factor
        keep = jnp.logical_or(i != j, causal)
        return scores, keep

    def row_stats(i):
        def visit(j, state):
            def update(st):
                top, total = st
                scores, keep = scores_of(i, j)
                scores = jnp.where(keep, scores, NEGATIVE_FILL)
                top_new = jnp.maximum(top, jnp.max(scores, axis=-1))
                probs = jnp.where(keep, jnp.exp(scores - top_new[..., None]), 0.0)
                return top_new, total * jnp.exp(top - top_new) + jnp.sum(probs, axis=-1)
            return lax.cond(seen[i, j] > 0, update, lambda st: st, state)

        start_index = (jnp.full((KEY_HEADS, QUERY_PER_KV, MASK_TILE), NEGATIVE_FILL, jnp.float32), jnp.zeros((KEY_HEADS, QUERY_PER_KV, MASK_TILE), jnp.float32))
        top, total = lax.fori_loop(0, TREE_TILES, visit, start_index)
        return top + jnp.log(total)

    lse_all = lax.map(row_stats, jnp.arange(TREE_TILES))

    def row_grads(i, carry):
        delta = jnp.sum(gradient_grouped5[i] * output_grouped5[i], axis=-1).transpose(1, 2, 0)

        def visit(j, inner):
            def update(st):
                query_gradient, key_gradient, value_gradient = st
                scores, keep = scores_of(i, j)
                probs = jnp.where(keep, jnp.exp(scores - lse_all[i][..., None]), 0.0)
                p16 = lax.optimization_barrier(probs.astype(jnp.bfloat16)).astype(jnp.float32)
                value_gradient = value_gradient.at[j].add(jnp.einsum('gnij,ignd->jgd', p16, gradient_grouped5[i], precision=high))
                dprobs = jnp.einsum('ignd,jgd->gnij', gradient_grouped5[i], value_tensor4[j], precision=high)
                ds = probs * (dprobs - delta[..., None])
                ds16 = lax.optimization_barrier(ds.astype(jnp.bfloat16)).astype(jnp.float32)
                query_gradient = query_gradient.at[i].add(jnp.einsum('gnij,jgd->ignd', ds16, key_tensor4[j], precision=high) * scale_factor)
                key_gradient = key_gradient.at[j].add(jnp.einsum('gnij,ignd->jgd', ds16, query_grouped5[i], precision=high) * scale_factor)
                return query_gradient, key_gradient, value_gradient
            return lax.cond(seen[i, j] > 0, update, lambda st: st, inner)

        return lax.cond(trained[i], lambda c: lax.fori_loop(0, TREE_TILES, visit, c), lambda c: c, carry)

    start_index = (jnp.zeros((TREE_TILES, MASK_TILE, KEY_HEADS, QUERY_PER_KV, HEAD_WIDTH), jnp.float32),
             jnp.zeros((TREE_TILES, MASK_TILE, KEY_HEADS, HEAD_WIDTH), jnp.float32),
             jnp.zeros((TREE_TILES, MASK_TILE, KEY_HEADS, HEAD_WIDTH), jnp.float32))
    query_gradient, key_gradient, value_gradient = lax.fori_loop(0, TREE_TILES, row_grads, start_index)
    return query_gradient.reshape(TREE_TOKENS, QUERY_HEADS * HEAD_WIDTH), key_gradient.reshape(TREE_TOKENS, KEY_HEADS * HEAD_WIDTH), value_gradient.reshape(TREE_TOKENS, KEY_HEADS * HEAD_WIDTH)


def reference(query, key, value, output, output_gradient, parent, owner):
    norm = (PROMPT_TREES * TREE_TOKENS) ** -0.5
    query_rows, key_rows, values = [], [], []
    bias_q = jnp.zeros((QUERY_HEADS * HEAD_WIDTH,), jnp.float32)
    key_bias_term = jnp.zeros((KEY_HEADS * HEAD_WIDTH,), jnp.float32)
    value_bias_term = jnp.zeros((KEY_HEADS * HEAD_WIDTH,), jnp.float32)
    for tree in range(PROMPT_TREES):
        tile_at, seen = tree_tables(parent[tree], owner[tree])
        trained = tile_at >= PROMPT_TILES
        query_gradient, key_gradient, value_gradient = one_tree(query[tree], key[tree], value[tree], output[tree], output_gradient[tree], seen, trained)
        bias_q = bias_q + jnp.sum(query_gradient, axis=0)
        key_bias_term = key_bias_term + jnp.sum(key_gradient, axis=0)
        value_bias_term = value_bias_term + jnp.sum(value_gradient, axis=0)
        query_rows.append(query_gradient.astype(jnp.bfloat16))
        key_rows.append(key_gradient.astype(jnp.bfloat16))
        values.append(value_gradient.astype(jnp.bfloat16))
    return (jnp.stack(query_rows), jnp.stack(key_rows), jnp.stack(values), bias_q * norm, key_bias_term * norm, value_bias_term * norm)
```

```python
import functools

import jax
import jax.numpy as jnp
from jax import lax
from jax.experimental import pallas as pl
from jax.experimental.pallas import tpu as pltpu
from jax.sharding import PartitionSpec as P

HEAD_WIDTH = 128
SCALE = HEAD_WIDTH**-0.5
LOG2E = 1.4426950408889634
NEGATIVE_FILL = -1e30
BY_LAST = (((1,), (1,)), ((), ()))
f32, bf16 = jnp.float32, jnp.bfloat16


def head_grads(parts, group, q_ref, g_ref, o_ref, kv_refs, dq_ref, sums, sq_ref):
    for total in sums:
        total[...] = jnp.zeros_like(total)

    def widen(row, first, fill):
        if not first:
            return row
        return jnp.concatenate([jnp.full((row.shape[0], first), fill, f32), row], axis=1)

    def one_head(h, carry):
        cols = pl.ds(pl.multiple_of(h * HEAD_WIDTH, HEAD_WIDTH), HEAD_WIDTH)
        qh, gh, oh = q_ref[:, cols], g_ref[:, cols], o_ref[:, cols]
        delta = jnp.sum((gh.astype(f32) * oh.astype(f32)).T, axis=0, keepdims=True)
        scores = []
        for b, k0, kn, q0, diagonal in parts:
            s = lax.dot_general(
                kv_refs[b][0, k0 : k0 + kn, :], qh[q0:], BY_LAST, preferred_element_type=f32
            )
            if diagonal:
                rows = k0 + lax.broadcasted_iota(jnp.int32, s.shape, 0)
                across = q0 + lax.broadcasted_iota(jnp.int32, s.shape, 1)
                s = jnp.where(rows <= across, s, NEGATIVE_FILL)
            scores.append(s)
        top = None
        for (b, k0, kn, q0, diagonal), s in zip(parts, scores):
            m = widen(jnp.max(s, axis=0, keepdims=True), q0, NEGATIVE_FILL)
            top = m if top is None else jnp.maximum(top, m)
        top = top * (SCALE * LOG2E)
        exps, total = [], None
        for (b, k0, kn, q0, diagonal), s in zip(parts, scores):
            e = jnp.exp2(s * (SCALE * LOG2E) - top[:, q0:])
            exps.append(e)
            t = widen(jnp.sum(e, axis=0, keepdims=True), q0, 0.0)
            total = t if total is None else total + t
        inverse = 1.0 / total
        dq_t = None
        for (b, k0, kn, q0, diagonal), e in zip(parts, exps):
            keys, values = kv_refs[b][0, k0 : k0 + kn, :], kv_refs[b][1, k0 : k0 + kn, :]
            p = e * inverse[:, q0:]
            dp = lax.dot_general(values, gh[q0:], BY_LAST, preferred_element_type=f32)
            ds = (p * (dp - delta[:, q0:])).astype(bf16)
            sums[b][1, k0 : k0 + kn, :] += jnp.dot(
                p.astype(bf16), gh[q0:], preferred_element_type=f32
            )
            sums[b][0, k0 : k0 + kn, :] += jnp.dot(ds, qh[q0:], preferred_element_type=f32)
            add = widen(jnp.dot(keys.T, ds, preferred_element_type=f32), q0, 0.0)
            dq_t = add if dq_t is None else dq_t + add
        dq = dq_t.T * SCALE
        dq_ref[:, cols] = dq.astype(bf16)
        sq_ref[:, cols] = jnp.sum(dq, axis=0, keepdims=True)
        return carry

    lax.fori_loop(0, group, one_head, 0)


def grads_kernel(
    group, prompts, mode_ref, q_ref, g_ref, o_ref, own, prompt, before,
    dq_ref, own_out, prompt_out, before_out, sq_ref, skv_ref, own_sum, prompt_sum, before_sum,
):
    tile = q_ref.shape[0]
    half = tile // 2
    kv_refs = [own, before] + [prompt.at[i] for i in range(prompts)]
    sums = [own_sum, before_sum] + [prompt_sum.at[i] for i in range(prompts)]
    parts = [(0, 0, half, 0, True), (0, half, half, half, True)]
    parts += [(2 + i, 0, tile, 0, False) for i in range(prompts)]
    mode = mode_ref[0]
    rest = (group, q_ref, g_ref, o_ref, kv_refs, dq_ref, sums, sq_ref)

    @pl.when(mode == 1)
    def _():
        head_grads(parts, *rest)

    @pl.when(mode == 2)
    def _():
        head_grads(parts + [(1, 0, tile, 0, False)], *rest)

    @pl.when(mode == 0)
    def _():
        dq_ref[...] = jnp.zeros_like(dq_ref)
        sq_ref[...] = jnp.zeros_like(sq_ref)
        for total in sums:
            total[...] = jnp.zeros_like(total)

    def put(out, total):
        dk, dv = total[0] * SCALE, total[1]
        out[0] = dk.astype(out.dtype)
        out[1] = dv.astype(out.dtype)
        return jnp.sum(dk, axis=0, keepdims=True), jnp.sum(dv, axis=0, keepdims=True)

    pairs = [put(own_out, own_sum), put(before_out, before_sum)]
    pairs += [put(prompt_out.at[i], prompt_sum.at[i]) for i in range(prompts)]
    skv_ref[0] = functools.reduce(jnp.add, [k for k, _ in pairs])
    skv_ref[1] = functools.reduce(jnp.add, [v for _, v in pairs])


def block_grads(mode, q, g, o, own, prompt, before):
    tile, q_width = q.shape
    width = own.shape[2]
    heads = width // HEAD_WIDTH
    group = q_width // width
    prompts = prompt.shape[0]
    q_spec = pl.BlockSpec((tile, group * HEAD_WIDTH), lambda h, m: (0, h))
    kv_spec = pl.BlockSpec((2, tile, HEAD_WIDTH), lambda h, m: (0, 0, h))
    p_spec = pl.BlockSpec((prompts, 2, tile, HEAD_WIDTH), lambda h, m: (0, 0, 0, h))
    pair = (2, tile, HEAD_WIDTH)
    return pl.pallas_call(
        functools.partial(grads_kernel, group, prompts),
        grid_spec=pltpu.PrefetchScalarGridSpec(
            num_scalar_prefetch=1,
            grid=(heads,),
            in_specs=[q_spec, q_spec, q_spec, kv_spec, p_spec, kv_spec],
            out_specs=[
                q_spec, kv_spec, p_spec, kv_spec,
                pl.BlockSpec((1, group * HEAD_WIDTH), lambda h, m: (0, h)),
                pl.BlockSpec((2, 1, HEAD_WIDTH), lambda h, m: (0, 0, h)),
            ],
            scratch_shapes=[
                pltpu.VMEM(pair, f32), pltpu.VMEM((prompts, *pair), f32), pltpu.VMEM(pair, f32)
            ],
        ),
        out_shape=[
            jax.ShapeDtypeStruct((tile, q_width), bf16),
            jax.ShapeDtypeStruct((2, tile, width), f32),
            jax.ShapeDtypeStruct((prompts, 2, tile, width), bf16),
            jax.ShapeDtypeStruct((2, tile, width), bf16),
            jax.ShapeDtypeStruct((1, q_width), f32),
            jax.ShapeDtypeStruct((2, 1, width), f32),
        ],
        compiler_params=pltpu.CompilerParams(vmem_limit_bytes=50 * 2**20),
    )(mode, q, g, o, own, prompt, before)


def pick(vector, index):
    spots = jnp.arange(vector.shape[0], dtype=jnp.int32)
    return jnp.sum(jnp.where(spots == index, vector, 0), axis=0)


def shared(chunk, count, me):
    routes = [[(i, (i + d) % count) for i in range(count)] for d in range(1, count)]
    arrived = [chunk] + [lax.ppermute(chunk, "ctx", route) for route in routes]
    arrived = jnp.stack(arrived)
    return jnp.take(arrived, (me - jnp.arange(count)) % count, axis=0)


def swapped(array, partner_bits, count):
    def swap(d):
        return lambda a: lax.ppermute(a, "ctx", [(i, i ^ d) for i in range(count)])

    return lax.switch(partner_bits, [lambda a: a] + [swap(d) for d in range(1, count)], array)


def on_device(query, key, value, output, output_gradient, parent, owner):
    count = lax.axis_size("ctx")
    trees = lax.axis_size("dp")
    me = lax.axis_index("ctx")
    tile = query.shape[1]
    width = key.shape[2]
    prompts = count // 8
    chunk_rows = 2 * tile // count
    parent, owner = parent[0], owner[0]
    spots = jnp.arange(count, dtype=jnp.int32)

    my_tile = pick(spots, jnp.argmax(owner == me))
    my_parent = pick(parent, my_tile)
    answers = my_tile >= prompts
    second = jnp.logical_and(answers, my_parent >= prompts)
    child = jnp.sum(jnp.where(parent == my_tile, spots, 0))
    first = jnp.logical_and(answers, child > 0)
    partner = jnp.where(second, pick(owner, my_parent), jnp.where(first, pick(owner, child), me))
    mode = jnp.where(second, 2, jnp.where(answers, 1, 0)).astype(jnp.int32)

    own = jnp.stack([key[0], value[0]])
    chunks = lax.all_to_all(own.reshape(count, chunk_rows, width), "ctx", 0, 0)
    mine = jnp.stack(
        [lax.dynamic_index_in_dim(chunks, owner[t], 0, keepdims=False) for t in range(prompts)]
    )
    prompt = shared(mine, count, me).transpose(1, 0, 2, 3).reshape(prompts, 2, tile, width)
    before = swapped(own, me ^ partner, count)

    dq, own_part, prompt_part, before_part, sum_q, sum_kv = block_grads(
        mode[None], query[0], output_gradient[0], output[0], own, prompt, before
    )

    sums = jnp.concatenate([sum_q.reshape(-1), sum_kv.reshape(-1)])
    devices = count * trees
    d = 1
    while d < devices:
        sums = sums + lax.ppermute(sums, ("ctx", "dp"), [(i, i ^ d) for i in range(devices)])
        d *= 2

    after = swapped(before_part, me ^ partner, count)
    parts = prompt_part.reshape(prompts, count, chunk_rows, width).transpose(1, 0, 2, 3)
    parts = lax.all_to_all(parts, "ctx", 0, 0)
    total = jnp.sum(parts.astype(f32), axis=0).astype(bf16)
    total = shared(total, count, me).transpose(1, 0, 2, 3).reshape(prompts, 2, tile, width)
    total = lax.dynamic_index_in_dim(
        total, jnp.minimum(my_tile, prompts - 1), 0, keepdims=False
    ).astype(f32)
    extra = jnp.where(answers, jnp.where(first, after.astype(f32), 0.0), total)
    grads = (own_part + extra).astype(bf16)

    norm = (trees * count * tile) ** -0.5
    sums = sums * norm
    q_width = query.shape[2]
    return (
        dq[None],
        grads[0][None],
        grads[1][None],
        sums[:q_width],
        sums[q_width : q_width + width],
        sums[q_width + width :],
    )


def solution(mesh):
    rows = P("dp", "ctx", "head")
    return jax.shard_map(
        on_device,
        mesh=mesh,
        in_specs=(rows, rows, rows, rows, rows, P("dp", None), P("dp", None)),
        out_specs=(rows, rows, rows, P("head"), P("head"), P("head")),
        check_vma=False,
    )
```

```python
import functools

import jax
import jax.numpy as jnp
from jax import lax
from jax.experimental import pallas as pl
from jax.experimental.pallas import tpu as pltpu
from jax.sharding import PartitionSpec as P

HEAD_WIDTH = 128
SCALE = HEAD_WIDTH**-0.5
TO_LOG2 = SCALE * 1.4426950408889634
NEGATIVE_FILL = -1e30
BY_LAST = (((1,), (1,)), ((), ()))
STAGES = (2, 2)
f32, bf16 = jnp.float32, jnp.bfloat16


def widened(row, first, fill):
    if not first:
        return row
    return jnp.concatenate([jnp.full((row.shape[0], first), fill, f32), row], axis=1)


def added(total, term):
    return term if total is None else total + term


def columns(h):
    return pl.ds(pl.multiple_of(h * HEAD_WIDTH, HEAD_WIDTH), HEAD_WIDTH)


def diagonal_scores(keys, qh, k0, q0):
    s = lax.dot_general(keys, qh, BY_LAST, preferred_element_type=f32)
    rows = k0 + lax.broadcasted_iota(jnp.int32, s.shape, 0)
    across = q0 + lax.broadcasted_iota(jnp.int32, s.shape, 1)
    return jnp.where(rows <= across, s, NEGATIVE_FILL)


def halves(tile):
    half = tile // 2
    return [(0, half, 0), (half, half, half)]


def over_keys(a, fn):
    return fn(a, axis=0, keepdims=True)


def own_stats_kernel(mode_ref, q_ref, g_ref, o_ref, k_ref, top_ref, total_ref, delta_ref):
    tile = q_ref.shape[0]
    group = q_ref.shape[1] // HEAD_WIDTH

    def one_head(h, carry):
        cols = columns(h)
        qh, gh, oh = q_ref[:, cols], g_ref[:, cols], o_ref[:, cols]
        delta_ref[0, pl.ds(h, 1), :] = over_keys((gh.astype(f32) * oh.astype(f32)).T, jnp.sum)
        scores = [
            diagonal_scores(k_ref[k0 : k0 + kn], qh[q0:], k0, q0) for k0, kn, q0 in halves(tile)
        ]
        top = None
        for (k0, kn, q0), s in zip(halves(tile), scores):
            m = widened(over_keys(s, jnp.max), q0, NEGATIVE_FILL)
            top = m if top is None else jnp.maximum(top, m)
        top = top * TO_LOG2
        total = None
        for (k0, kn, q0), s in zip(halves(tile), scores):
            e = jnp.exp2(s * TO_LOG2 - top[:, q0:])
            total = added(total, widened(over_keys(e, jnp.sum), q0, 0.0))
        top_ref[0, pl.ds(h, 1), :] = top
        total_ref[0, pl.ds(h, 1), :] = total
        return carry

    @pl.when(mode_ref[0] > 0)
    def _():
        lax.fori_loop(0, group, one_head, 0, unroll=True)

    @pl.when(mode_ref[0] == 0)
    def _():
        for ref in (top_ref, total_ref, delta_ref):
            ref[...] = jnp.zeros_like(ref)


def far_kernel(
    mode_ref, q_ref, g_ref, top_ref, total_ref, delta_ref, far_ref,
    dq_ref, lse_ref, far_out, skv_ref, sums, turned,
):
    tile = q_ref.shape[0]
    group = q_ref.shape[1] // HEAD_WIDTH
    count, others = far_ref.shape[:2]
    mode = mode_ref[0]
    blocks = [
        [far_ref[:, i, kv].reshape(tile, HEAD_WIDTH) for kv in range(2)] for i in range(others)
    ]

    def work(used):
        sums[...] = jnp.zeros_like(sums)
        for b in range(used):
            turned[b] = blocks[b][0].T

        def one_head(h, carry):
            cols = columns(h)
            row = pl.ds(h, 1)
            qh, gh = q_ref[:, cols], g_ref[:, cols]
            scores = [
                lax.dot_general(blocks[b][0], qh, BY_LAST, preferred_element_type=f32)
                for b in range(used)
            ]
            own_top = top_ref[0, row, :]
            top = own_top
            for s in scores:
                top = jnp.maximum(top, over_keys(s, jnp.max) * TO_LOG2)
            total = total_ref[0, row, :] * jnp.exp2(own_top - top)
            exps = []
            for s in scores:
                exps.append(jnp.exp2(s * TO_LOG2 - top))
                total = total + over_keys(exps[-1], jnp.sum)
            inverse = 1.0 / total
            lse_ref[0, row, :] = top + jnp.log2(total)
            delta = delta_ref[0, row, :]
            dq_t = None
            for b in range(used):
                p = exps[b] * inverse
                dp = lax.dot_general(blocks[b][1], gh, BY_LAST, preferred_element_type=f32)
                ds = (p * (dp - delta)).astype(bf16)
                sums[b, 1] += jnp.dot(p.astype(bf16), gh, preferred_element_type=f32)
                sums[b, 0] += jnp.dot(ds, qh, preferred_element_type=f32)
                dq_t = added(dq_t, jnp.dot(turned[b], ds, preferred_element_type=f32))
            dq_ref[:, cols] = dq_t.T
            return carry

        lax.fori_loop(0, group, one_head, 0, unroll=True)

    @pl.when(mode == 1)
    def _():
        work(others - 1)

    @pl.when(mode == 2)
    def _():
        work(others)

    @pl.when(mode == 0)
    def _():
        for ref in (dq_ref, lse_ref, sums):
            ref[...] = jnp.zeros_like(ref)

    over = [0.0, 0.0]
    for kv in range(2):
        for b in range(others):
            grad = sums[b, kv] * SCALE if kv == 0 else sums[b, kv]
            over[kv] += over_keys(grad, jnp.sum)
            far_out[:, b, kv] = grad.astype(bf16).reshape(count, tile // count, HEAD_WIDTH)
        skv_ref[kv] = over[kv]


def own_grads_kernel(
    mode_ref, q_ref, g_ref, lse_ref, delta_ref, k_ref, v_ref, dq_part,
    dq_ref, own_out, sq_ref, skv_ref, sums, turned,
):
    tile = q_ref.shape[0]
    group = q_ref.shape[1] // HEAD_WIDTH

    def one_head(h, carry):
        cols = columns(h)
        row = pl.ds(h, 1)
        qh, gh = q_ref[:, cols], g_ref[:, cols]
        lse, delta = lse_ref[0, row, :], delta_ref[0, row, :]
        dq_t = None
        for k0, kn, q0 in halves(tile):
            s = diagonal_scores(k_ref[k0 : k0 + kn], qh[q0:], k0, q0)
            p = jnp.exp2(s * TO_LOG2 - lse[:, q0:])
            dp = lax.dot_general(v_ref[k0 : k0 + kn], gh[q0:], BY_LAST, preferred_element_type=f32)
            ds = (p * (dp - delta[:, q0:])).astype(bf16)
            sums[1, k0 : k0 + kn] += jnp.dot(p.astype(bf16), gh[q0:], preferred_element_type=f32)
            sums[0, k0 : k0 + kn] += jnp.dot(ds, qh[q0:], preferred_element_type=f32)
            add = jnp.dot(turned[:, k0 : k0 + kn], ds, preferred_element_type=f32)
            dq_t = added(dq_t, widened(add, q0, 0.0))
        dq = (dq_t.T + dq_part[:, cols]) * SCALE
        dq_ref[:, cols] = dq.astype(bf16)
        sq_ref[:, cols] = over_keys(dq, jnp.sum)
        return carry

    sums[...] = jnp.zeros_like(sums)

    @pl.when(mode_ref[0] > 0)
    def _():
        turned[...] = k_ref[...].T
        lax.fori_loop(0, group, one_head, 0, unroll=True)

    @pl.when(mode_ref[0] == 0)
    def _():
        dq_ref[...] = jnp.zeros_like(dq_ref)
        sq_ref[...] = jnp.zeros_like(sq_ref)

    for kv in range(2):
        grad = sums[kv] * SCALE if kv == 0 else sums[kv]
        own_out[kv] = grad
        skv_ref[kv] = over_keys(grad, jnp.sum)


def call(kernel, heads, first, units, in_specs, out_specs, out_shape, scratch, args, aliases={}):
    tile = args[1].shape[0]
    group = in_specs[0].block_shape[1] // HEAD_WIDTH
    macs = int(heads * group * units * tile * tile * HEAD_WIDTH)
    return pl.pallas_call(
        kernel,
        grid_spec=pltpu.PrefetchScalarGridSpec(
            num_scalar_prefetch=1, grid=(heads,), in_specs=in_specs, out_specs=out_specs,
            scratch_shapes=scratch,
        ),
        out_shape=out_shape,
        input_output_aliases=aliases,
        cost_estimate=pl.CostEstimate(
            flops=4 * macs, bytes_accessed=8 * tile * group * heads * HEAD_WIDTH, transcendentals=0
        ),
        compiler_params=pltpu.CompilerParams(vmem_limit_bytes=50 * 2**20),
    )(*args)


def specs(tile, group, first):
    q = pl.BlockSpec((tile, group * HEAD_WIDTH), lambda h, m: (0, first + h))
    kv = pl.BlockSpec((tile, HEAD_WIDTH), lambda h, m: (0, first + h))
    row = pl.BlockSpec((1, group, tile), lambda h, m: (first + h, 0, 0))
    return q, kv, row


def own_stats(mode, q, g, o, keys):
    tile, q_width = q.shape
    heads = keys.shape[1] // HEAD_WIDTH
    group = q_width // keys.shape[1]
    q_spec, kv_spec, row = specs(tile, group, 0)
    stat = jax.ShapeDtypeStruct((heads, group, tile), f32)
    return call(
        own_stats_kernel, heads, 0, 0.75, [q_spec, q_spec, q_spec, kv_spec], [row] * 3, [stat] * 3,
        [], (mode, q, g, o, keys),
    )


def far_grads(first, mode, q, g, stats, far, made):
    tile, q_width = q.shape
    group = stats[0].shape[1]
    count, others, _, rows, part = far.shape
    q_spec, kv_spec, row = specs(tile, group, first)
    far_spec = pl.BlockSpec((count, others, 2, rows, HEAD_WIDTH), lambda h, m: (0, 0, 0, 0, h))
    whole = pl.BlockSpec(memory_space=pl.ANY)

    def kernel(*refs):
        far_kernel(*refs[:7], *refs[7 + len(made) :])

    return call(
        kernel, part // HEAD_WIDTH, first, 5 * others,
        [q_spec, q_spec, row, row, row, far_spec] + [whole] * len(made),
        [q_spec, row, far_spec, pl.BlockSpec((2, 1, HEAD_WIDTH), lambda h, m: (0, 0, h))],
        [
            jax.ShapeDtypeStruct((tile, q_width), f32),
            jax.ShapeDtypeStruct(stats[0].shape, f32),
            jax.ShapeDtypeStruct(far.shape, bf16),
            jax.ShapeDtypeStruct((2, 1, part), f32),
        ],
        [
            pltpu.VMEM((others, 2, tile, HEAD_WIDTH), f32),
            pltpu.VMEM((others, HEAD_WIDTH, tile), bf16),
        ],
        (mode, q, g, *stats, far, *made),
        {7 + i: i for i in range(len(made))},
    )


def own_grads(mode, q, g, lse, delta, keys, values, dq):
    tile, q_width = q.shape
    width = keys.shape[1]
    heads = width // HEAD_WIDTH
    group = q_width // width
    q_spec, kv_spec, row = specs(tile, group, 0)
    return call(
        own_grads_kernel, heads, 0, 3.75, [q_spec, q_spec, row, row, kv_spec, kv_spec, q_spec],
        [q_spec, pl.BlockSpec((2, tile, HEAD_WIDTH), lambda h, m: (0, 0, h)),
         pl.BlockSpec((1, group * HEAD_WIDTH), lambda h, m: (0, h)),
         pl.BlockSpec((2, 1, HEAD_WIDTH), lambda h, m: (0, 0, h))],
        [
            jax.ShapeDtypeStruct((tile, q_width), bf16),
            jax.ShapeDtypeStruct((2, tile, width), f32),
            jax.ShapeDtypeStruct((1, q_width), f32),
            jax.ShapeDtypeStruct((2, 1, width), f32),
        ],
        [pltpu.VMEM((2, tile, HEAD_WIDTH), f32), pltpu.VMEM((HEAD_WIDTH, tile), bf16)],
        (mode, q, g, lse, delta, keys, values, dq),
    )


def pass_on_kernel(sources_ref, chunks, *outs):
    count, others = outs[0].shape[:2]
    for j in range(count):
        for i in range(others):
            source = sources_ref[j * others + i]
            end = 0
            for out in outs:
                first, end = end, end + out.shape[4]
                out[j, i] = chunks[source, :, :, first:end]


def passed_on(sources, chunks, stages):
    count, _, rows, _ = chunks.shape
    others = sources.shape[1]
    in_vmem = pl.BlockSpec(memory_space=pltpu.VMEM)
    return pl.pallas_call(
        pass_on_kernel,
        grid_spec=pltpu.PrefetchScalarGridSpec(
            num_scalar_prefetch=1, in_specs=[in_vmem], out_specs=[in_vmem] * len(stages)
        ),
        out_shape=[
            jax.ShapeDtypeStruct((count, others, 2, rows, n * HEAD_WIDTH), bf16) for n in stages
        ],
        compiler_params=pltpu.CompilerParams(vmem_limit_bytes=50 * 2**20),
    )(sources.reshape(-1), chunks)


def collect_kernel(wanted_ref, *refs):
    *parts, terms, out = refs
    count, others, _, rows, _ = parts[0].shape
    prompts = others - 1
    for i, part in enumerate(parts):
        first = 2 * i * rows
        totals = [part[0, t].astype(f32) for t in range(prompts)]
        for t in range(prompts):
            for source in range(1, count):
                totals[t] += part[source, t].astype(f32)

        for j in range(count):
            w = wanted_ref[j]
            for t in range(prompts):

                @pl.when(w == t)
                def _():
                    for kv in range(2):
                        out[j, first + kv * rows : first + (kv + 1) * rows] = totals[t][kv].astype(bf16)

            @pl.when(w >= prompts)
            def _():
                for kv in range(2):
                    out[j, first + kv * rows : first + (kv + 1) * rows] = part[w - prompts, prompts, kv]

    for j in range(count):
        out[j, 2 * len(parts) * rows :] = terms[...]


def collected(wanted, parts, terms):
    count, _, _, rows, width = parts[0].shape
    shape = (count, 2 * len(parts) * rows + terms.shape[0], width)
    return pl.pallas_call(
        collect_kernel,
        grid_spec=pltpu.PrefetchScalarGridSpec(
            num_scalar_prefetch=1,
            in_specs=[pl.BlockSpec(memory_space=pltpu.VMEM)] * (len(parts) + 1),
            out_specs=pl.BlockSpec(memory_space=pltpu.VMEM),
        ),
        out_shape=jax.ShapeDtypeStruct(shape, bf16),
        compiler_params=pltpu.CompilerParams(vmem_limit_bytes=50 * 2**20),
    )(wanted, *parts, terms)


def pick(vector, index):
    spots = jnp.arange(vector.shape[-1], dtype=jnp.int32)
    return jnp.sum(jnp.where(spots == index, vector, 0), axis=-1)


def tree_routes(parent, owner, prompts):
    count = parent.shape[0]
    spots = jnp.arange(count, dtype=jnp.int32)
    tile_at = jnp.sum(jnp.where(owner[None] == spots[:, None], spots[None], 0), axis=1)
    above = pick(parent[None], tile_at[:, None])
    second = jnp.logical_and(tile_at >= prompts, above >= prompts)
    before = jnp.where(second, pick(owner[None], above[:, None]), -1)
    after = jnp.sum(jnp.where(before[None] == spots[:, None], spots[None] + 1, 0), axis=1) - 1
    return tile_at, before, after


def on_device(query, key, value, output, output_gradient, parent, owner):
    count = lax.axis_size("ctx")
    trees = lax.axis_size("dp")
    me = lax.axis_index("ctx")
    query, key, value, output, upstream = (a[0] for a in (query, key, value, output, output_gradient))
    tile, q_width = query.shape
    width = key.shape[1]
    heads = width // HEAD_WIDTH
    prompts = count // 8
    rows = tile // count
    owner = owner[0]
    tile_at, before_at, after_at = tree_routes(parent[0], owner, prompts)
    mine, before_me, after_me = (pick(a, me) for a in (tile_at, before_at, after_at))
    mode = jnp.where(mine < prompts, 0, jnp.where(before_me < 0, 1, 2)).astype(jnp.int32)[None]

    def exchange(a):
        return lax.all_to_all(a, "ctx", 0, 0)

    sources = jnp.concatenate(
        [jnp.broadcast_to(owner[:prompts], (count, prompts)), jnp.maximum(before_at, 0)[:, None]], axis=1
    )
    stages = STAGES if sum(STAGES) == heads else (1,) * heads
    ends = [sum(stages[: i + 1]) * HEAD_WIDTH for i in range(len(stages))]
    chunks = exchange(jnp.stack([a.reshape(count, rows, width) for a in (key, value)], axis=1))
    stats = own_stats(mode, query, upstream, output, key)
    chunks, stats = lax.optimization_barrier((chunks, stats))
    far = [exchange(block) for block in passed_on(sources, chunks, stages)]

    made, parts, sums_kv = [], [], []
    for end, n, block in zip(ends, stages, far):
        *made, part, skv = far_grads(end // HEAD_WIDTH - n, mode, query, upstream, stats, block, made)
        parts.append(exchange(part))
        sums_kv.append(skv)
    dq, lse = made
    parts[0], lse = lax.optimization_barrier((parts[0], lse))
    dq, own, sq, own_skv = own_grads(mode, query, upstream, lse, stats[2], key, value, dq)

    sums = jnp.concatenate([sq.reshape(-1), (jnp.concatenate(sums_kv, axis=2) + own_skv).reshape(-1)])
    routes = [(i, i ^ 1) for i in range(trees)]
    sums = sums + lax.ppermute(sums, "dp", routes)
    high = lax.reduce_precision(sums, 8, 7)
    low = (sums - high).astype(bf16)
    high = high.astype(bf16)
    part = stages[0] * HEAD_WIDTH
    extra = -(-2 * sums.shape[0] // (16 * part)) * 16
    terms = jnp.concatenate([high, low])
    terms = jnp.pad(terms, (0, extra * part - terms.shape[0])).reshape(extra, part)

    wanted = jnp.where(tile_at < prompts, tile_at, prompts + jnp.maximum(after_at, 0))
    last = exchange(collected(wanted, parts, terms))
    takes = jnp.logical_or(mine < prompts, after_me >= 0)

    terms = last[:, -extra:].reshape(count, -1).astype(f32)
    size = sums.shape[0]
    sums = jnp.sum(terms[:, :size] + terms[:, size : 2 * size], axis=0) * (trees * count * tile) ** -0.5
    outs = []
    for kv in range(2):
        add = [
            last[:, (2 * i + kv) * rows : (2 * i + kv + 1) * rows].reshape(tile, part)
            for i in range(len(stages))
        ]
        add = jnp.where(takes, jnp.concatenate(add, axis=1), 0)
        outs.append((own[kv] + add.astype(f32)).astype(bf16))
    return (
        dq[None],
        outs[0][None],
        outs[1][None],
        sums[:q_width],
        sums[q_width : q_width + width],
        sums[q_width + width :],
    )


def solution(mesh):
    rows = P("dp", "ctx", "head")
    return jax.shard_map(
        on_device,
        mesh=mesh,
        in_specs=(rows, rows, rows, rows, rows, P("dp", None), P("dp", None)),
        out_specs=(rows, rows, rows, P("head"), P("head"), P("head")),
        check_vma=False,
    )
```

```python
import functools

import jax
import jax.numpy as jnp
from jax import lax
from jax.experimental import pallas as pl
from jax.experimental.pallas import tpu as pltpu
from jax.sharding import PartitionSpec as P

HEAD_WIDTH = 128
SCALE = HEAD_WIDTH**-0.5
TO_LOG2 = SCALE * 1.4426950408889634
NEGATIVE_FILL = -1e30
BY_LAST = (((1,), (1,)), ((), ()))
STAGES = (2, 2)
TERM_ROWS = 16
f32, bf16 = jnp.float32, jnp.bfloat16


def widened(row, first, fill):
    if not first:
        return row
    return jnp.concatenate([jnp.full((row.shape[0], first), fill, f32), row], axis=1)


def added(total, term):
    return term if total is None else total + term


def columns(h):
    return pl.ds(pl.multiple_of(h * HEAD_WIDTH, HEAD_WIDTH), HEAD_WIDTH)


def diagonal_scores(keys, qh, k0, q0):
    s = lax.dot_general(keys, qh, BY_LAST, preferred_element_type=f32)
    rows = k0 + lax.broadcasted_iota(jnp.int32, s.shape, 0)
    across = q0 + lax.broadcasted_iota(jnp.int32, s.shape, 1)
    return jnp.where(rows <= across, s, NEGATIVE_FILL)


def halves(tile):
    half = tile // 2
    return [(0, half, 0), (half, half, half)]


def over_keys(a, fn):
    return fn(a, axis=0, keepdims=True)


def own_stats_kernel(mode_ref, q_ref, g_ref, o_ref, k_ref, top_ref, total_ref, delta_ref):
    tile = q_ref.shape[0]
    group = q_ref.shape[1] // HEAD_WIDTH

    def one_head(h, carry):
        cols = columns(h)
        qh, gh, oh = q_ref[:, cols], g_ref[:, cols], o_ref[:, cols]
        delta_ref[0, pl.ds(h, 1), :] = over_keys((gh.astype(f32) * oh.astype(f32)).T, jnp.sum)
        scores = [
            diagonal_scores(k_ref[k0 : k0 + kn], qh[q0:], k0, q0) for k0, kn, q0 in halves(tile)
        ]
        top = None
        for (k0, kn, q0), s in zip(halves(tile), scores):
            m = widened(over_keys(s, jnp.max), q0, NEGATIVE_FILL)
            top = m if top is None else jnp.maximum(top, m)
        top = top * TO_LOG2
        total = None
        for (k0, kn, q0), s in zip(halves(tile), scores):
            e = jnp.exp2(s * TO_LOG2 - top[:, q0:])
            total = added(total, widened(over_keys(e, jnp.sum), q0, 0.0))
        top_ref[0, pl.ds(h, 1), :] = top
        total_ref[0, pl.ds(h, 1), :] = total
        return carry

    @pl.when(mode_ref[0] > 0)
    def _():
        lax.fori_loop(0, group, one_head, 0, unroll=True)

    @pl.when(mode_ref[0] == 0)
    def _():
        for ref in (top_ref, total_ref, delta_ref):
            ref[...] = jnp.zeros_like(ref)


def far_kernel(
    mode_ref, q_ref, g_ref, top_ref, total_ref, delta_ref, far_refs,
    dq_ref, lse_ref, far_out, skv_ref, sums, turned,
):
    tile = q_ref.shape[0]
    group = q_ref.shape[1] // HEAD_WIDTH
    by_distance = len(far_refs) > 1
    chunks = far_refs if by_distance else [far_refs[0].at[i] for i in range(far_refs[0].shape[0])]
    count, others = len(chunks), chunks[0].shape[0]
    rows = tile // count
    mode, me = mode_ref[0], mode_ref[1]
    blocks = [
        [jnp.concatenate([ref[i, kv] for ref in chunks], axis=0) for kv in range(2)]
        for i in range(others)
    ]

    def work(used):
        sums[...] = jnp.zeros_like(sums)
        for b in range(used):
            turned[b] = blocks[b][0].T

        def one_head(h, carry):
            cols = columns(h)
            row = pl.ds(h, 1)
            qh, gh = q_ref[:, cols], g_ref[:, cols]
            scores = [
                lax.dot_general(blocks[b][0], qh, BY_LAST, preferred_element_type=f32)
                for b in range(used)
            ]
            own_top = top_ref[0, row, :]
            top = own_top
            for s in scores:
                top = jnp.maximum(top, over_keys(s, jnp.max) * TO_LOG2)
            total = total_ref[0, row, :] * jnp.exp2(own_top - top)
            exps = []
            for s in scores:
                exps.append(jnp.exp2(s * TO_LOG2 - top))
                total = total + over_keys(exps[-1], jnp.sum)
            inverse = 1.0 / total
            lse_ref[0, row, :] = top + jnp.log2(total)
            delta = delta_ref[0, row, :]
            dq_t = None
            for b in range(used):
                p = exps[b] * inverse
                dp = lax.dot_general(blocks[b][1], gh, BY_LAST, preferred_element_type=f32)
                ds = (p * (dp - delta)).astype(bf16)
                sums[b, 1] += jnp.dot(p.astype(bf16), gh, preferred_element_type=f32)
                sums[b, 0] += jnp.dot(ds, qh, preferred_element_type=f32)
                dq_t = added(dq_t, jnp.dot(turned[b], ds, preferred_element_type=f32))
            dq_ref[:, cols] = dq_t.T
            return carry

        lax.fori_loop(0, group, one_head, 0, unroll=True)

    @pl.when(mode == 1)
    def _():
        work(others - 1)

    @pl.when(mode == 2)
    def _():
        work(others)

    @pl.when(mode == 0)
    def _():
        for ref in (dq_ref, lse_ref, sums):
            ref[...] = jnp.zeros_like(ref)

    over = [0.0, 0.0]
    for kv in range(2):
        for b in range(others):
            grad = sums[b, kv] * SCALE if kv == 0 else sums[b, kv]
            over[kv] += over_keys(grad, jnp.sum)
            grad = grad.astype(bf16)
            for d in range(count):
                at = around(me, -d, count) if by_distance else d
                far_out[at, b, kv] = grad[d * rows : (d + 1) * rows]
        skv_ref[kv] = over[kv]


def own_grads_kernel(
    mode_ref, q_ref, g_ref, lse_ref, delta_ref, k_ref, v_ref, dq_part,
    dq_ref, own_out, sq_ref, skv_ref, sums, turned,
):
    tile = q_ref.shape[0]
    group = q_ref.shape[1] // HEAD_WIDTH

    def one_head(h, carry):
        cols = columns(h)
        row = pl.ds(h, 1)
        qh, gh = q_ref[:, cols], g_ref[:, cols]
        lse, delta = lse_ref[0, row, :], delta_ref[0, row, :]
        dq_t = None
        for k0, kn, q0 in halves(tile):
            s = diagonal_scores(k_ref[k0 : k0 + kn], qh[q0:], k0, q0)
            p = jnp.exp2(s * TO_LOG2 - lse[:, q0:])
            dp = lax.dot_general(v_ref[k0 : k0 + kn], gh[q0:], BY_LAST, preferred_element_type=f32)
            ds = (p * (dp - delta[:, q0:])).astype(bf16)
            sums[1, k0 : k0 + kn] += jnp.dot(p.astype(bf16), gh[q0:], preferred_element_type=f32)
            sums[0, k0 : k0 + kn] += jnp.dot(ds, qh[q0:], preferred_element_type=f32)
            add = jnp.dot(turned[:, k0 : k0 + kn], ds, preferred_element_type=f32)
            dq_t = added(dq_t, widened(add, q0, 0.0))
        dq = (dq_t.T + dq_part[:, cols]) * SCALE
        dq_ref[:, cols] = dq.astype(bf16)
        sq_ref[:, cols] = over_keys(dq, jnp.sum)
        return carry

    sums[...] = jnp.zeros_like(sums)

    @pl.when(mode_ref[0] > 0)
    def _():
        turned[...] = k_ref[...].T
        lax.fori_loop(0, group, one_head, 0, unroll=True)

    @pl.when(mode_ref[0] == 0)
    def _():
        dq_ref[...] = jnp.zeros_like(dq_ref)
        sq_ref[...] = jnp.zeros_like(sq_ref)

    for kv in range(2):
        grad = sums[kv] * SCALE if kv == 0 else sums[kv]
        own_out[kv] = grad
        skv_ref[kv] = over_keys(grad, jnp.sum)


def call(kernel, heads, first, units, in_specs, out_specs, out_shape, scratch, args, aliases={}):
    tile = args[1].shape[0]
    group = in_specs[0].block_shape[1] // HEAD_WIDTH
    macs = int(heads * group * units * tile * tile * HEAD_WIDTH)
    return pl.pallas_call(
        kernel,
        grid_spec=pltpu.PrefetchScalarGridSpec(
            num_scalar_prefetch=1, grid=(heads,), in_specs=in_specs, out_specs=out_specs,
            scratch_shapes=scratch,
        ),
        out_shape=out_shape,
        input_output_aliases=aliases,
        cost_estimate=pl.CostEstimate(
            flops=4 * macs, bytes_accessed=8 * tile * group * heads * HEAD_WIDTH, transcendentals=0
        ),
        compiler_params=pltpu.CompilerParams(vmem_limit_bytes=50 * 2**20),
    )(*args)


def specs(tile, group, first):
    q = pl.BlockSpec((tile, group * HEAD_WIDTH), lambda h, m: (0, first + h))
    kv = pl.BlockSpec((tile, HEAD_WIDTH), lambda h, m: (0, first + h))
    row = pl.BlockSpec((1, group, tile), lambda h, m: (first + h, 0, 0))
    return q, kv, row


def own_stats(mode, q, g, o, keys):
    tile, q_width = q.shape
    heads = keys.shape[1] // HEAD_WIDTH
    group = q_width // keys.shape[1]
    q_spec, kv_spec, row = specs(tile, group, 0)
    stat = jax.ShapeDtypeStruct((heads, group, tile), f32)
    return call(
        own_stats_kernel, heads, 0, 0.75, [q_spec, q_spec, q_spec, kv_spec], [row] * 3, [stat] * 3,
        [], (mode, q, g, o, keys),
    )


def far_grads(first, mode, q, g, stats, far, made):
    tile, q_width = q.shape
    group = stats[0].shape[1]
    given = len(far)
    others, _, rows, part = far[0].shape[-4:]
    count = tile // rows
    q_spec, kv_spec, row = specs(tile, group, first)
    chunk_spec = pl.BlockSpec((others, 2, rows, HEAD_WIDTH), lambda h, m: (0, 0, 0, h))
    far_spec = pl.BlockSpec((count, others, 2, rows, HEAD_WIDTH), lambda h, m: (0, 0, 0, 0, h))
    whole = pl.BlockSpec(memory_space=pl.ANY)

    def kernel(*refs):
        far_kernel(*refs[:6], refs[6 : 6 + given], *refs[6 + given + len(made) :])

    return call(
        kernel, part // HEAD_WIDTH, first, 5 * others,
        [q_spec, q_spec, row, row, row]
        + ([far_spec] if given == 1 else [chunk_spec] * given) + [whole] * len(made),
        [q_spec, row, far_spec, pl.BlockSpec((2, 1, HEAD_WIDTH), lambda h, m: (0, 0, h))],
        [
            jax.ShapeDtypeStruct((tile, q_width), f32),
            jax.ShapeDtypeStruct(stats[0].shape, f32),
            jax.ShapeDtypeStruct((count, others, 2, rows, part), bf16),
            jax.ShapeDtypeStruct((2, 1, part), f32),
        ],
        [
            pltpu.VMEM((others, 2, tile, HEAD_WIDTH), f32),
            pltpu.VMEM((others, HEAD_WIDTH, tile), bf16),
        ],
        (mode, q, g, *stats, *far, *made),
        {6 + given + i: i for i in range(len(made))},
    )


def own_grads(mode, q, g, lse, delta, keys, values, dq):
    tile, q_width = q.shape
    width = keys.shape[1]
    heads = width // HEAD_WIDTH
    group = q_width // width
    q_spec, kv_spec, row = specs(tile, group, 0)
    return call(
        own_grads_kernel, heads, 0, 3.75, [q_spec, q_spec, row, row, kv_spec, kv_spec, q_spec],
        [q_spec, pl.BlockSpec((2, tile, HEAD_WIDTH), lambda h, m: (0, 0, h)),
         pl.BlockSpec((1, group * HEAD_WIDTH), lambda h, m: (0, h)),
         pl.BlockSpec((2, 1, HEAD_WIDTH), lambda h, m: (0, 0, h))],
        [
            jax.ShapeDtypeStruct((tile, q_width), bf16),
            jax.ShapeDtypeStruct((2, tile, width), f32),
            jax.ShapeDtypeStruct((1, q_width), f32),
            jax.ShapeDtypeStruct((2, 1, width), f32),
        ],
        [pltpu.VMEM((2, tile, HEAD_WIDTH), f32), pltpu.VMEM((HEAD_WIDTH, tile), bf16)],
        (mode, q, g, lse, delta, keys, values, dq),
    )


def around(me, d, count):
    return lax.rem(me + (count + d), count)


def chunk_kernel(me_ref, key, value, *outs):
    count, rows = len(outs), outs[0].shape[1]
    for d, out in enumerate(outs):
        at = pl.ds(pl.multiple_of(around(me_ref[0], d, count) * rows, rows), rows)
        out[0] = key[at]
        out[1] = value[at]


def pass_on_kernel(sources_ref, *refs):
    count = refs[-1].shape[0]
    chunks, outs, table = refs[:count], refs[count:-1], refs[-1]
    others = outs[0].shape[0]
    me = sources_ref[count * others]
    for d in range(count):
        table[around(me, -d, count)] = chunks[d][...]
    for d in range(count):
        to = around(me, d, count)
        for i in range(others):
            source = sources_ref[to * others + i]
            end = outs[0].shape[3]
            outs[d][i] = table[source, :, :, :end]
            for out in outs[count:]:
                first, end = end, end + out.shape[4]
                out[to, i] = table[source, :, :, first:end]


def collect_kernel(wanted_ref, sums, *refs):
    count, others, _, rows, part = refs[0].shape
    parts, outs = refs[:-count], refs[-count:]
    prompts = others - 1
    me = wanted_ref[count]
    for n, source_parts in enumerate(parts):
        totals = [source_parts[0, t].astype(f32) for t in range(prompts)]
        for t in range(prompts):
            for source in range(1, count):
                totals[t] += source_parts[source, t].astype(f32)
        for d, out in enumerate(outs):
            w = wanted_ref[around(me, d, count)]
            first = 2 * n * rows
            for t in range(prompts):

                @pl.when(w == t)
                def _():
                    for kv in range(2):
                        out[first + kv * rows : first + (kv + 1) * rows] = totals[t][kv].astype(bf16)

            @pl.when(w >= prompts)
            def _():
                for kv in range(2):
                    out[first + kv * rows : first + (kv + 1) * rows] = source_parts[
                        w - prompts, prompts, kv
                    ]

    high = sums[...].astype(bf16)
    low = (sums[...] - high.astype(f32)).astype(bf16)
    first = 2 * len(parts) * rows
    for out in outs:
        out[first : first + TERM_ROWS] = high
        out[first + TERM_ROWS :] = low


def finish_kernel(norm, at_ref, own, *refs):
    chunks, outs, total, table = refs[:-4], refs[-4:-2], refs[-2], refs[-1]
    count = len(chunks)
    part = chunks[0].shape[1]
    rows = own.shape[1] // count
    stages = own.shape[2] // part
    for d in range(count):
        source = around(at_ref[0], -d, count)
        at = pl.ds(pl.multiple_of(source * rows, rows), rows)
        for n in range(stages):
            cols = slice(n * part, (n + 1) * part)
            for kv in range(2):
                first = (2 * n + kv) * rows
                add = jnp.where(at_ref[1] == 1, chunks[d][first : first + rows].astype(f32), 0.0)
                outs[kv][at, cols] = (own[kv, at, cols] + add).astype(bf16)
        first = 2 * stages * rows
        high, low = chunks[d][first : first + TERM_ROWS], chunks[d][first + TERM_ROWS :]
        table[source] = high.astype(f32) + low.astype(f32)
    over = table[0]
    for i in range(1, count):
        over += table[i]
    total[...] = over * norm


def layout(kernel, scalars, args, out_shape, scratch=()):
    in_vmem = pl.BlockSpec(memory_space=pltpu.VMEM)
    return pl.pallas_call(
        kernel,
        grid_spec=pltpu.PrefetchScalarGridSpec(
            num_scalar_prefetch=1, in_specs=[in_vmem] * len(args), out_specs=[in_vmem] * len(out_shape),
            scratch_shapes=list(scratch),
        ),
        out_shape=out_shape,
        compiler_params=pltpu.CompilerParams(vmem_limit_bytes=50 * 2**20),
    )(scalars, *args)


def pick(vector, index):
    spots = jnp.arange(vector.shape[-1], dtype=jnp.int32)
    return jnp.sum(jnp.where(spots == index, vector, 0), axis=-1)


def tree_routes(parent, owner, prompts):
    count = parent.shape[0]
    spots = jnp.arange(count, dtype=jnp.int32)
    tile_at = jnp.sum(jnp.where(owner[None] == spots[:, None], spots[None], 0), axis=1)
    above = pick(parent[None], tile_at[:, None])
    second = jnp.logical_and(tile_at >= prompts, above >= prompts)
    before = jnp.where(second, pick(owner[None], above[:, None]), -1)
    after = jnp.sum(jnp.where(before[None] == spots[:, None], spots[None] + 1, 0), axis=1) - 1
    return tile_at, before, after


def on_device(query, key, value, output, output_gradient, parent, owner):
    count = lax.axis_size("ctx")
    trees = lax.axis_size("dp")
    me = lax.axis_index("ctx")
    query, key, value, output, upstream = (a[0] for a in (query, key, value, output, output_gradient))
    tile, q_width = query.shape
    width = key.shape[1]
    heads = width // HEAD_WIDTH
    prompts = count // 8
    rows = tile // count
    owner = owner[0]
    tile_at, before_at, after_at = tree_routes(parent[0], owner, prompts)
    mine, before_me, after_me = (pick(a, me) for a in (tile_at, before_at, after_at))
    mode = jnp.where(mine < prompts, 0, jnp.where(before_me < 0, 1, 2))
    mode = jnp.stack([mode, me]).astype(jnp.int32)

    def exchange(a):
        return lax.all_to_all(a, "ctx", 0, 0)

    sources = jnp.concatenate(
        [jnp.broadcast_to(owner[:prompts], (count, prompts)), jnp.maximum(before_at, 0)[:, None]], axis=1
    )
    stages = STAGES if sum(STAGES) == heads else (1,) * heads
    ends = [sum(stages[: i + 1]) * HEAD_WIDTH for i in range(len(stages))]
    routes = [[(i, (i + d) % count) for i in range(count)] for d in range(count)]

    def around_ring(by_distance):
        sent = [lax.ppermute(a, "ctx", route) for a, route in zip(by_distance[1:], routes[1:])]
        return [by_distance[0], *sent]

    here = me.astype(jnp.int32)[None]
    chunk = jax.ShapeDtypeStruct((2, rows, width), bf16)
    chunks = around_ring(layout(chunk_kernel, here, (key, value), [chunk] * count))
    stats = own_stats(mode, query, upstream, output, key)
    chunks, stats = lax.optimization_barrier((chunks, stats))
    sizes = [(prompts + 1, 2, rows, n * HEAD_WIDTH) for n in stages]
    pieces = layout(
        pass_on_kernel, jnp.concatenate([sources.reshape(-1), here]), chunks,
        [jax.ShapeDtypeStruct(sizes[0], bf16)] * count
        + [jax.ShapeDtypeStruct((count, *size), bf16) for size in sizes[1:]],
        [pltpu.VMEM((count, 2, rows, width), bf16)],
    )
    far = [around_ring(pieces[:count])]
    if len(stages) > 1:
        pieces, far = lax.optimization_barrier((pieces[count:], far))
        far += [[exchange(piece)] for piece in pieces]

    made, parts, sums_kv = [], [], []
    for end, n, block in zip(ends, stages, far):
        *made, part, skv = far_grads(end // HEAD_WIDTH - n, mode, query, upstream, stats, block, made)
        parts.append(exchange(part))
        sums_kv.append(skv)
    dq, lse = made
    parts[0], lse = lax.optimization_barrier((parts[0], lse))
    dq, own, sq, own_skv = own_grads(mode, query, upstream, lse, stats[2], key, value, dq)

    part = stages[0] * HEAD_WIDTH
    sums = jnp.concatenate([sq.reshape(-1), (jnp.concatenate(sums_kv, axis=2) + own_skv).reshape(-1)])
    sums = sums + lax.ppermute(sums, "dp", [(i, i ^ 1) for i in range(trees)])
    size = sums.shape[0]
    sums = jnp.pad(sums, (0, TERM_ROWS * part - size)).reshape(TERM_ROWS, part)
    wanted = jnp.where(tile_at < prompts, tile_at, prompts + jnp.maximum(after_at, 0))
    chunk = jax.ShapeDtypeStruct((2 * len(stages) * rows + 2 * TERM_ROWS, part), bf16)
    last = around_ring(
        layout(collect_kernel, jnp.concatenate([wanted, here]), (sums, *parts), [chunk] * count)
    )
    takes = jnp.logical_or(mine < prompts, after_me >= 0)
    *outs, sums = layout(
        functools.partial(finish_kernel, (trees * count * tile) ** -0.5),
        jnp.stack([me, takes.astype(me.dtype)]).astype(jnp.int32), (own, *last),
        [jax.ShapeDtypeStruct((tile, width), bf16)] * 2 + [jax.ShapeDtypeStruct(sums.shape, f32)],
        [pltpu.VMEM((count, TERM_ROWS, part), f32)],
    )
    sums = sums.reshape(-1)
    return (
        dq[None],
        outs[0][None],
        outs[1][None],
        sums[:q_width],
        sums[q_width : q_width + width],
        sums[q_width + width : size],
    )


def solution(mesh):
    rows = P("dp", "ctx", "head")
    return jax.shard_map(
        on_device,
        mesh=mesh,
        in_specs=(rows, rows, rows, rows, rows, P("dp", None), P("dp", None)),
        out_specs=(rows, rows, rows, P("head"), P("head"), P("head")),
        check_vma=False,
    )
```

```python
import functools

import jax
import jax.numpy as jnp
from jax import lax
from jax.experimental import pallas as pl
from jax.experimental.pallas import tpu as pltpu
from jax.sharding import PartitionSpec as P

HEAD_WIDTH = 128
SCALE = HEAD_WIDTH**-0.5
TO_LOG2 = SCALE * 1.4426950408889634
NEGATIVE_FILL = -1e30
BY_LAST = (((1,), (1,)), ((), ()))
STAGES = (2, 2)
TERM_ROWS = 16
f32, bf16 = jnp.float32, jnp.bfloat16


def widened(row, first, fill):
    if not first:
        return row
    return jnp.concatenate([jnp.full((row.shape[0], first), fill, f32), row], axis=1)


def added(total, term):
    return term if total is None else total + term


def columns(h):
    return pl.ds(pl.multiple_of(h * HEAD_WIDTH, HEAD_WIDTH), HEAD_WIDTH)


def diagonal_scores(keys, qh, k0, q0):
    s = lax.dot_general(keys, qh, BY_LAST, preferred_element_type=f32)
    rows = k0 + lax.broadcasted_iota(jnp.int32, s.shape, 0)
    across = q0 + lax.broadcasted_iota(jnp.int32, s.shape, 1)
    return jnp.where(rows <= across, s, NEGATIVE_FILL)


def halves(tile):
    half = tile // 2
    return [(0, half, 0), (half, half, half)]


def over_keys(a, fn):
    return fn(a, axis=0, keepdims=True)


def own_stats_kernel(mode_ref, q_ref, g_ref, o_ref, k_ref, top_ref, total_ref, delta_ref):
    tile = q_ref.shape[0]
    group = q_ref.shape[1] // HEAD_WIDTH

    def one_head(h, carry):
        cols = columns(h)
        qh, gh, oh = q_ref[:, cols], g_ref[:, cols], o_ref[:, cols]
        delta_ref[0, pl.ds(h, 1), :] = over_keys((gh.astype(f32) * oh.astype(f32)).T, jnp.sum)
        scores = [
            diagonal_scores(k_ref[k0 : k0 + kn], qh[q0:], k0, q0) for k0, kn, q0 in halves(tile)
        ]
        top = None
        for (k0, kn, q0), s in zip(halves(tile), scores):
            m = widened(over_keys(s, jnp.max), q0, NEGATIVE_FILL)
            top = m if top is None else jnp.maximum(top, m)
        top = top * TO_LOG2
        total = None
        for (k0, kn, q0), s in zip(halves(tile), scores):
            e = jnp.exp2(s * TO_LOG2 - top[:, q0:])
            total = added(total, widened(over_keys(e, jnp.sum), q0, 0.0))
        top_ref[0, pl.ds(h, 1), :] = top
        total_ref[0, pl.ds(h, 1), :] = total
        return carry

    @pl.when(mode_ref[0] > 0)
    def _():
        lax.fori_loop(0, group, one_head, 0, unroll=True)

    @pl.when(mode_ref[0] == 0)
    def _():
        for ref in (top_ref, total_ref, delta_ref):
            ref[...] = jnp.zeros_like(ref)


def far_kernel(
    mode_ref, q_ref, g_ref, top_ref, total_ref, delta_ref, far_refs,
    dq_ref, lse_ref, far_out, skv_ref, sums, turned,
):
    tile = q_ref.shape[0]
    group = q_ref.shape[1] // HEAD_WIDTH
    by_distance = len(far_refs) > 1
    chunks = far_refs if by_distance else [far_refs[0].at[i] for i in range(far_refs[0].shape[0])]
    count, others = len(chunks), chunks[0].shape[0]
    rows = tile // count
    mode, me = mode_ref[0], mode_ref[1]
    blocks = [
        [jnp.concatenate([ref[i, kv] for ref in chunks], axis=0) for kv in range(2)]
        for i in range(others)
    ]

    def work(used):
        sums[...] = jnp.zeros_like(sums)
        for b in range(used):
            turned[b] = blocks[b][0].T

        def one_head(h, carry):
            cols = columns(h)
            row = pl.ds(h, 1)
            qh, gh = q_ref[:, cols], g_ref[:, cols]
            scores = [
                lax.dot_general(blocks[b][0], qh, BY_LAST, preferred_element_type=f32)
                for b in range(used)
            ]
            own_top = top_ref[0, row, :]
            top = own_top
            for s in scores:
                top = jnp.maximum(top, over_keys(s, jnp.max) * TO_LOG2)
            total = total_ref[0, row, :] * jnp.exp2(own_top - top)
            exps = []
            for s in scores:
                exps.append(jnp.exp2(s * TO_LOG2 - top))
                total = total + over_keys(exps[-1], jnp.sum)
            inverse = 1.0 / total
            lse_ref[0, row, :] = top + jnp.log2(total)
            delta = delta_ref[0, row, :]
            dq_t = None
            for b in range(used):
                p = exps[b] * inverse
                dp = lax.dot_general(blocks[b][1], gh, BY_LAST, preferred_element_type=f32)
                ds = (p * (dp - delta)).astype(bf16)
                sums[b, 1] += jnp.dot(p.astype(bf16), gh, preferred_element_type=f32)
                sums[b, 0] += jnp.dot(ds, qh, preferred_element_type=f32)
                dq_t = added(dq_t, jnp.dot(turned[b], ds, preferred_element_type=f32))
            dq_ref[:, cols] = dq_t.T
            return carry

        lax.fori_loop(0, group, one_head, 0, unroll=True)

    @pl.when(mode == 1)
    def _():
        work(others - 1)

    @pl.when(mode == 2)
    def _():
        work(others)

    @pl.when(mode == 0)
    def _():
        for ref in (dq_ref, lse_ref, sums):
            ref[...] = jnp.zeros_like(ref)

    over = [0.0, 0.0]
    for kv in range(2):
        for b in range(others):
            grad = sums[b, kv] * SCALE if kv == 0 else sums[b, kv]
            over[kv] += over_keys(grad, jnp.sum)
            grad = grad.astype(bf16)
            for d in range(count):
                at = around(me, -d, count) if by_distance else d
                far_out[at, b, kv] = grad[d * rows : (d + 1) * rows]
        skv_ref[kv] = over[kv]


def own_grads_kernel(
    mode_ref, q_ref, g_ref, lse_ref, delta_ref, k_ref, v_ref, dq_part,
    dq_ref, own_out, sq_ref, skv_ref, sums, turned,
):
    tile = q_ref.shape[0]
    group = q_ref.shape[1] // HEAD_WIDTH

    def one_head(h, carry):
        cols = columns(h)
        row = pl.ds(h, 1)
        qh, gh = q_ref[:, cols], g_ref[:, cols]
        lse, delta = lse_ref[0, row, :], delta_ref[0, row, :]
        dq_t = None
        for k0, kn, q0 in halves(tile):
            s = diagonal_scores(k_ref[k0 : k0 + kn], qh[q0:], k0, q0)
            p = jnp.exp2(s * TO_LOG2 - lse[:, q0:])
            dp = lax.dot_general(v_ref[k0 : k0 + kn], gh[q0:], BY_LAST, preferred_element_type=f32)
            ds = (p * (dp - delta[:, q0:])).astype(bf16)
            sums[1, k0 : k0 + kn] += jnp.dot(p.astype(bf16), gh[q0:], preferred_element_type=f32)
            sums[0, k0 : k0 + kn] += jnp.dot(ds, qh[q0:], preferred_element_type=f32)
            add = jnp.dot(turned[:, k0 : k0 + kn], ds, preferred_element_type=f32)
            dq_t = added(dq_t, widened(add, q0, 0.0))
        dq = (dq_t.T + dq_part[:, cols]) * SCALE
        dq_ref[:, cols] = dq.astype(bf16)
        sq_ref[:, cols] = over_keys(dq, jnp.sum)
        return carry

    sums[...] = jnp.zeros_like(sums)

    @pl.when(mode_ref[0] > 0)
    def _():
        turned[...] = k_ref[...].T
        lax.fori_loop(0, group, one_head, 0, unroll=True)

    @pl.when(mode_ref[0] == 0)
    def _():
        dq_ref[...] = jnp.zeros_like(dq_ref)
        sq_ref[...] = jnp.zeros_like(sq_ref)

    for kv in range(2):
        grad = sums[kv] * SCALE if kv == 0 else sums[kv]
        own_out[kv] = grad
        skv_ref[kv] = over_keys(grad, jnp.sum)


def call(kernel, heads, first, units, in_specs, out_specs, out_shape, scratch, args, aliases={}):
    tile = args[1].shape[0]
    group = in_specs[0].block_shape[1] // HEAD_WIDTH
    macs = int(heads * group * units * tile * tile * HEAD_WIDTH)
    return pl.pallas_call(
        kernel,
        grid_spec=pltpu.PrefetchScalarGridSpec(
            num_scalar_prefetch=1, grid=(heads,), in_specs=in_specs, out_specs=out_specs,
            scratch_shapes=scratch,
        ),
        out_shape=out_shape,
        input_output_aliases=aliases,
        cost_estimate=pl.CostEstimate(
            flops=4 * macs, bytes_accessed=8 * tile * group * heads * HEAD_WIDTH, transcendentals=0
        ),
        compiler_params=pltpu.CompilerParams(vmem_limit_bytes=50 * 2**20),
    )(*args)


def specs(tile, group, first):
    q = pl.BlockSpec((tile, group * HEAD_WIDTH), lambda h, m: (0, first + h))
    kv = pl.BlockSpec((tile, HEAD_WIDTH), lambda h, m: (0, first + h))
    row = pl.BlockSpec((1, group, tile), lambda h, m: (first + h, 0, 0))
    return q, kv, row


def own_stats(mode, q, g, o, keys):
    tile, q_width = q.shape
    heads = keys.shape[1] // HEAD_WIDTH
    group = q_width // keys.shape[1]
    q_spec, kv_spec, row = specs(tile, group, 0)
    stat = jax.ShapeDtypeStruct((heads, group, tile), f32)
    return call(
        own_stats_kernel, heads, 0, 0.75, [q_spec, q_spec, q_spec, kv_spec], [row] * 3, [stat] * 3,
        [], (mode, q, g, o, keys),
    )


def far_grads(first, mode, q, g, stats, far, made):
    tile, q_width = q.shape
    group = stats[0].shape[1]
    given = len(far)
    others, _, rows, part = far[0].shape[-4:]
    count = tile // rows
    q_spec, kv_spec, row = specs(tile, group, first)
    chunk_spec = pl.BlockSpec((others, 2, rows, HEAD_WIDTH), lambda h, m: (0, 0, 0, h))
    far_spec = pl.BlockSpec((count, others, 2, rows, HEAD_WIDTH), lambda h, m: (0, 0, 0, 0, h))
    whole = pl.BlockSpec(memory_space=pl.ANY)

    def kernel(*refs):
        far_kernel(*refs[:6], refs[6 : 6 + given], *refs[6 + given + len(made) :])

    return call(
        kernel, part // HEAD_WIDTH, first, 5 * others,
        [q_spec, q_spec, row, row, row]
        + ([far_spec] if given == 1 else [chunk_spec] * given) + [whole] * len(made),
        [q_spec, row, far_spec, pl.BlockSpec((2, 1, HEAD_WIDTH), lambda h, m: (0, 0, h))],
        [
            jax.ShapeDtypeStruct((tile, q_width), f32),
            jax.ShapeDtypeStruct(stats[0].shape, f32),
            jax.ShapeDtypeStruct((count, others, 2, rows, part), bf16),
            jax.ShapeDtypeStruct((2, 1, part), f32),
        ],
        [
            pltpu.VMEM((others, 2, tile, HEAD_WIDTH), f32),
            pltpu.VMEM((others, HEAD_WIDTH, tile), bf16),
        ],
        (mode, q, g, *stats, *far, *made),
        {6 + given + i: i for i in range(len(made))},
    )


def own_grads(mode, q, g, lse, delta, keys, values, dq):
    tile, q_width = q.shape
    width = keys.shape[1]
    heads = width // HEAD_WIDTH
    group = q_width // width
    q_spec, kv_spec, row = specs(tile, group, 0)
    return call(
        own_grads_kernel, heads, 0, 3.75, [q_spec, q_spec, row, row, kv_spec, kv_spec, q_spec],
        [q_spec, pl.BlockSpec((2, tile, HEAD_WIDTH), lambda h, m: (0, 0, h)),
         pl.BlockSpec((1, group * HEAD_WIDTH), lambda h, m: (0, h)),
         pl.BlockSpec((2, 1, HEAD_WIDTH), lambda h, m: (0, 0, h))],
        [
            jax.ShapeDtypeStruct((tile, q_width), bf16),
            jax.ShapeDtypeStruct((2, tile, width), f32),
            jax.ShapeDtypeStruct((1, q_width), f32),
            jax.ShapeDtypeStruct((2, 1, width), f32),
        ],
        [pltpu.VMEM((2, tile, HEAD_WIDTH), f32), pltpu.VMEM((HEAD_WIDTH, tile), bf16)],
        (mode, q, g, lse, delta, keys, values, dq),
    )


def around(me, d, count):
    return lax.rem(me + (count + d), count)


def chunk_kernel(me_ref, key, value, *outs):
    count, rows = len(outs), outs[0].shape[1]
    for d, out in enumerate(outs):
        at = pl.ds(pl.multiple_of(around(me_ref[0], d, count) * rows, rows), rows)
        out[0] = key[at]
        out[1] = value[at]


def pass_on_kernel(sources_ref, *refs):
    count = refs[-1].shape[0]
    chunks, outs, table = refs[:count], refs[count:-1], refs[-1]
    others = outs[0].shape[0]
    me = sources_ref[count * others]
    for d in range(count):
        table[around(me, -d, count)] = chunks[d][...]
    for d in range(count):
        to = around(me, d, count)
        for i in range(others):
            source = sources_ref[to * others + i]
            end = outs[0].shape[3]
            outs[d][i] = table[source, :, :, :end]
            for out in outs[count:]:
                first, end = end, end + out.shape[4]
                out[to, i] = table[source, :, :, first:end]


def collect_kernel(wanted_ref, sums, *refs):
    count, others, _, rows, part = refs[0].shape
    parts, outs = refs[:-count], refs[-count:]
    prompts = others - 1
    me = wanted_ref[count]
    for n, source_parts in enumerate(parts):
        totals = [source_parts[0, t].astype(f32) for t in range(prompts)]
        for t in range(prompts):
            for source in range(1, count):
                totals[t] += source_parts[source, t].astype(f32)
        for d, out in enumerate(outs):
            w = wanted_ref[around(me, d, count)]
            first = 2 * n * rows
            for t in range(prompts):

                @pl.when(w == t)
                def _():
                    for kv in range(2):
                        out[first + kv * rows : first + (kv + 1) * rows] = totals[t][kv].astype(bf16)

            @pl.when(w >= prompts)
            def _():
                for kv in range(2):
                    out[first + kv * rows : first + (kv + 1) * rows] = source_parts[
                        w - prompts, prompts, kv
                    ]

    high = sums[...].astype(bf16)
    low = (sums[...] - high.astype(f32)).astype(bf16)
    first = 2 * len(parts) * rows
    for out in outs:
        out[first : first + TERM_ROWS] = high
        out[first + TERM_ROWS :] = low


def finish_kernel(norm, at_ref, own, *refs):
    chunks, outs, total, table = refs[:-4], refs[-4:-2], refs[-2], refs[-1]
    count = len(chunks)
    part = chunks[0].shape[1]
    rows = own.shape[1] // count
    stages = own.shape[2] // part
    for d in range(count):
        source = around(at_ref[0], -d, count)
        at = pl.ds(pl.multiple_of(source * rows, rows), rows)
        for n in range(stages):
            cols = slice(n * part, (n + 1) * part)
            for kv in range(2):
                first = (2 * n + kv) * rows
                add = jnp.where(at_ref[1] == 1, chunks[d][first : first + rows].astype(f32), 0.0)
                outs[kv][at, cols] = (own[kv, at, cols] + add).astype(bf16)
        first = 2 * stages * rows
        high, low = chunks[d][first : first + TERM_ROWS], chunks[d][first + TERM_ROWS :]
        table[source] = high.astype(f32) + low.astype(f32)
    over = table[0]
    for i in range(1, count):
        over += table[i]
    total[...] = over * norm


def layout(kernel, scalars, args, out_shape, scratch=()):
    in_vmem = pl.BlockSpec(memory_space=pltpu.VMEM)
    return pl.pallas_call(
        kernel,
        grid_spec=pltpu.PrefetchScalarGridSpec(
            num_scalar_prefetch=1, in_specs=[in_vmem] * len(args), out_specs=[in_vmem] * len(out_shape),
            scratch_shapes=list(scratch),
        ),
        out_shape=out_shape,
        compiler_params=pltpu.CompilerParams(vmem_limit_bytes=50 * 2**20),
    )(scalars, *args)


def pick(vector, index):
    spots = jnp.arange(vector.shape[-1], dtype=jnp.int32)
    return jnp.sum(jnp.where(spots == index, vector, 0), axis=-1)


def tree_routes(parent, owner, prompts):
    count = parent.shape[0]
    spots = jnp.arange(count, dtype=jnp.int32)
    tile_at = jnp.sum(jnp.where(owner[None] == spots[:, None], spots[None], 0), axis=1)
    above = pick(parent[None], tile_at[:, None])
    second = jnp.logical_and(tile_at >= prompts, above >= prompts)
    before = jnp.where(second, pick(owner[None], above[:, None]), -1)
    after = jnp.sum(jnp.where(before[None] == spots[:, None], spots[None] + 1, 0), axis=1) - 1
    return tile_at, before, after


def on_device(query, key, value, output, output_gradient, parent, owner):
    count = lax.axis_size("ctx")
    trees = lax.axis_size("dp")
    me = lax.axis_index("ctx")
    query, key, value, output, upstream = (a[0] for a in (query, key, value, output, output_gradient))
    tile, q_width = query.shape
    width = key.shape[1]
    heads = width // HEAD_WIDTH
    prompts = count // 8
    rows = tile // count
    owner = owner[0]
    tile_at, before_at, after_at = tree_routes(parent[0], owner, prompts)
    mine, before_me, after_me = (pick(a, me) for a in (tile_at, before_at, after_at))
    mode = jnp.where(mine < prompts, 0, jnp.where(before_me < 0, 1, 2))
    mode = jnp.stack([mode, me]).astype(jnp.int32)

    def exchange(a):
        return lax.all_to_all(a, "ctx", 0, 0)

    sources = jnp.concatenate(
        [jnp.broadcast_to(owner[:prompts], (count, prompts)), jnp.maximum(before_at, 0)[:, None]], axis=1
    )
    stages = STAGES if sum(STAGES) == heads else (1,) * heads
    ends = [sum(stages[: i + 1]) * HEAD_WIDTH for i in range(len(stages))]
    routes = [[(i, (i + d) % count) for i in range(count)] for d in range(count)]

    def around_ring(by_distance):
        arrived = list(by_distance)
        for d in sorted(range(1, count), key=lambda d: abs(2 * d - count)):
            arrived[d] = lax.ppermute(by_distance[d], "ctx", routes[d])
        return arrived

    here = me.astype(jnp.int32)[None]
    chunk = jax.ShapeDtypeStruct((2, rows, width), bf16)
    chunks = around_ring(layout(chunk_kernel, here, (key, value), [chunk] * count))
    stats = own_stats(mode, query, upstream, output, key)
    chunks, stats = lax.optimization_barrier((chunks, stats))
    sizes = [(prompts + 1, 2, rows, n * HEAD_WIDTH) for n in stages]
    pieces = layout(
        pass_on_kernel, jnp.concatenate([sources.reshape(-1), here]), chunks,
        [jax.ShapeDtypeStruct(sizes[0], bf16)] * count
        + [jax.ShapeDtypeStruct((count, *size), bf16) for size in sizes[1:]],
        [pltpu.VMEM((count, 2, rows, width), bf16)],
    )
    far = [around_ring(pieces[:count])]
    if len(stages) > 1:
        pieces, far = lax.optimization_barrier((pieces[count:], far))
        far += [[exchange(piece)] for piece in pieces]

    made, parts, sums_kv = [], [], []
    for end, n, block in zip(ends, stages, far):
        *made, part, skv = far_grads(end // HEAD_WIDTH - n, mode, query, upstream, stats, block, made)
        parts.append(exchange(part))
        sums_kv.append(skv)
    dq, lse = made
    parts[0], lse = lax.optimization_barrier((parts[0], lse))
    dq, own, sq, own_skv = own_grads(mode, query, upstream, lse, stats[2], key, value, dq)

    part = stages[0] * HEAD_WIDTH
    sums = jnp.concatenate([sq.reshape(-1), (jnp.concatenate(sums_kv, axis=2) + own_skv).reshape(-1)])
    sums = sums + lax.ppermute(sums, "dp", [(i, i ^ 1) for i in range(trees)])
    size = sums.shape[0]
    sums = jnp.pad(sums, (0, TERM_ROWS * part - size)).reshape(TERM_ROWS, part)
    wanted = jnp.where(tile_at < prompts, tile_at, prompts + jnp.maximum(after_at, 0))
    chunk = jax.ShapeDtypeStruct((2 * len(stages) * rows + 2 * TERM_ROWS, part), bf16)
    last = around_ring(
        layout(collect_kernel, jnp.concatenate([wanted, here]), (sums, *parts), [chunk] * count)
    )
    takes = jnp.logical_or(mine < prompts, after_me >= 0)
    *outs, sums = layout(
        functools.partial(finish_kernel, (trees * count * tile) ** -0.5),
        jnp.stack([me, takes.astype(me.dtype)]).astype(jnp.int32), (own, *last),
        [jax.ShapeDtypeStruct((tile, width), bf16)] * 2 + [jax.ShapeDtypeStruct(sums.shape, f32)],
        [pltpu.VMEM((count, TERM_ROWS, part), f32)],
    )
    sums = sums.reshape(-1)
    return (
        dq[None],
        outs[0][None],
        outs[1][None],
        sums[:q_width],
        sums[q_width : q_width + width],
        sums[q_width + width : size],
    )


def solution(mesh):
    rows = P("dp", "ctx", "head")
    return jax.shard_map(
        on_device,
        mesh=mesh,
        in_specs=(rows, rows, rows, rows, rows, P("dp", None), P("dp", None)),
        out_specs=(rows, rows, rows, P("head"), P("head"), P("head")),
        check_vma=False,
    )
```
